32 devices in a mesh: mode: 8 (over z, core), dom: 4 (over y, x).
Axes of the slice: x: 2, y: 2, z: 4, core: 2. Of those that a mesh axis runs over, the one named last changes fastest.
Arguments:
- velocity: float32 [3, 128, 2, 8192], P(None, 'mode', None, 'dom'), may hold values from -0.375 to 0.375
- vorticity: float32 [3, 128, 2, 8192], P(None, 'mode', None, 'dom'), may hold values from -0.375 to 0.375
- blocks: float32 [9, 64, 64], replicated, may hold values from -0.042 to 0.042
- nbr_ref: int32 [9, 128], P(None, 'dom'), may hold values from 0 to 47
- send_list: int32 [2, 32], P(None, 'dom'), may hold values from 0 to 31
Outputs:
- velocity_new: float32 [3, 128, 2, 8192], P(None, 'mode', None, 'dom')
The draws below stay inside these ranges and needn't reach their ends.
Inputs may be any that keep to these rules, and one draw needn't show every extreme that they name: nbr_ref indexes the extended list of the element's own partition; partitions form a cycle. send_list holds local element numbers of the partition that holds the entry.
All inputs are finite; a program needn't handle non-finite values.
Results may differ from the reference program's by a relative error of at most 0.0001.
Values sent between devices are 32-bit elements; how exact they have to be, the bound alone decides.
A program may use at most 64 MiB of HBM per device.

```python
import jax
import jax.numpy as jnp
from jax import lax

NP = 64
MODES = 128
NBR = 9
CHEB = 4
ELEM_DEV = 32
SEND = 8
ELEMS = 128
N_DOM = 4


def plant(values, key, low, top_value):
    index_at = [jax.random.randint(jax.random.fold_in(key, axis), (), 0, length) for axis, length in enumerate(values.shape)]
    widest = values.shape.index(max(values.shape))
    neighbour = index_at[:widest] + [(index_at[widest] + 1) % values.shape[widest]] + index_at[widest + 1:]
    return values.at[tuple(index_at)].set(low).at[tuple(neighbour)].set(top_value)


def block_scale(own_key, shape, split, low, high):
    def one(axis_at, shards_of):
        steps = jax.random.uniform(jax.random.fold_in(jax.random.fold_in(own_key, 6), axis_at), (shards_of,), jnp.float32, low / len(split), high / len(split))
        return jnp.repeat(jnp.exp(steps), shape[axis_at] // shards_of).reshape((-1,) + (1,) * (len(shape) - axis_at - 1))

    gain = one(*split[0])
    for cut in split[1:]:
        gain = gain * one(*cut)
    return gain


def normal_values(rng, dims, deviation, bound, split=(), held_as=jnp.bfloat16):
    drawn = deviation * jax.random.normal(rng, dims, jnp.float32)
    if split:
        drawn = drawn * block_scale(rng, dims, split, -0.22, 0.18)
    return jnp.clip(drawn, -bound, bound).astype(held_as)


def setup_inputs(seed: int = 0) -> dict:
    arg_keys = jax.random.split(jax.random.key(seed), 6)
    velocity = normal_values(arg_keys[0], (3, MODES, 2, ELEMS * NP), (1.0 / (2 * MODES) ** 0.5), 0.375, ((1, 8), (3, 4)), jnp.float32)
    vorticity = normal_values(arg_keys[1], (3, MODES, 2, ELEMS * NP), (1.0 / (2 * MODES) ** 0.5), 0.375, ((1, 8), (3, 4)), jnp.float32)
    blocks = normal_values(arg_keys[2], (NBR, NP, NP), (0.056 / NP ** 0.5), 0.042, (), jnp.float32)
    nbr_ref = plant(jax.random.randint(arg_keys[3], (NBR, ELEMS), 0, ELEM_DEV + 2 * SEND), jax.random.fold_in(arg_keys[3], 1), 0, (ELEM_DEV + 2 * SEND) - 1).astype(jnp.int32)
    send_list = plant(jax.random.randint(arg_keys[4], (2, N_DOM * SEND), 0, ELEM_DEV), jax.random.fold_in(arg_keys[4], 1), 0, ELEM_DEV - 1).astype(jnp.int32)
    return {"velocity": velocity, "vorticity": vorticity, "blocks": blocks, "nbr_ref": nbr_ref, "send_list": send_list}


def spanwise_tables(count):
    mode_ids = jnp.arange(count, dtype=jnp.int32)
    planes = jnp.arange(2 * count, dtype=jnp.int32)
    phase = (planes[:, None] * mode_ids[None, :]) % (2 * count)
    angle = (2.0 * jnp.pi / (2 * count)) * phase.astype(jnp.float32)
    weights = jnp.where(mode_ids == 0, 1.0, 2.0).astype(jnp.float32)
    inv_cos = weights[None, :] * jnp.cos(angle)
    inv_sin = weights[None, :] * jnp.sin(angle)
    back_cos = jnp.cos(angle).T / (2 * count)
    back_sin = -jnp.sin(angle).T / (2 * count)
    return inv_cos, inv_sin, back_cos, back_sin


def line_forcing(vel_lines, vort_lines, tables):
    inv_cos, inv_sin, back_cos, back_sin = tables
    highest = lax.Precision.HIGHEST

    def to_planes(field):
        return (jnp.einsum('zk,ckx->czx', inv_cos, field[:, :, 0], precision=highest)
                - jnp.einsum('zk,ckx->czx', inv_sin, field[:, :, 1], precision=highest))

    vel_planes = to_planes(vel_lines)
    vort_planes = to_planes(vort_lines)
    cross = jnp.stack([
        vel_planes[1] * vort_planes[2] - vel_planes[2] * vort_planes[1],
        vel_planes[2] * vort_planes[0] - vel_planes[0] * vort_planes[2],
        vel_planes[0] * vort_planes[1] - vel_planes[1] * vort_planes[0]])
    real_part = jnp.einsum('kz,czx->ckx', back_cos, cross, precision=highest)
    imag_part = jnp.einsum('kz,czx->ckx', back_sin, cross, precision=highest)
    return jnp.stack([real_part, imag_part], axis=2)


def unmerge(field):
    return jnp.swapaxes(field.reshape(3, MODES, 2, ELEMS, NP), 3, 4)


def remerge(field):
    return jnp.swapaxes(field, 3, 4).reshape(3, MODES, 2, ELEMS * NP)


def reference(velocity, vorticity, blocks, nbr_ref, send_list):
    highest = lax.Precision.HIGHEST
    tables = spanwise_tables(MODES)
    velocity = unmerge(velocity)
    vorticity = unmerge(vorticity)

    def one_point(pair):
        return line_forcing(pair[0], pair[1], tables)

    forcing = lax.map(one_point, (jnp.moveaxis(velocity, 3, 0), jnp.moveaxis(vorticity, 3, 0)))
    forcing = jnp.moveaxis(forcing, 0, 3)
    wavenum = jnp.arange(MODES, dtype=jnp.int32).astype(jnp.float32) / MODES
    inv_diag = (1.0 / (1.0 + 4.0 * wavenum * wavenum)).reshape(1, MODES, 1, 1, 1)
    element = jnp.arange(ELEMS, dtype=jnp.int32)
    partition = jnp.broadcast_to(element // ELEM_DEV, nbr_ref.shape)
    below = (partition - 1) % N_DOM
    above = (partition + 1) % N_DOM
    off_below = jnp.clip(nbr_ref - ELEM_DEV, 0, SEND - 1)
    off_above = jnp.clip(nbr_ref - ELEM_DEV - SEND, 0, SEND - 1)
    from_below = below * ELEM_DEV + send_list[0][below * SEND + off_below]
    from_above = above * ELEM_DEV + send_list[1][above * SEND + off_above]
    global_ids = jnp.where(nbr_ref < ELEM_DEV, partition * ELEM_DEV + nbr_ref,
                           jnp.where(nbr_ref < ELEM_DEV + SEND, from_below, from_above)).astype(jnp.int32)

    def apply_operator(field):
        total = jnp.zeros_like(field)
        for slot in range(blocks.shape[0]):
            picked = jnp.take(field, global_ids[slot], axis=4)
            total = total + jnp.einsum('pq,cmrqe->cmrpe', blocks[slot], picked, precision=highest)
        return field + inv_diag * total

    rhs = (velocity + forcing) * inv_diag
    solution = jnp.zeros_like(rhs)
    resid = rhs
    direction = rhs
    rho = 0.5
    for step in range(CHEB):
        solution = solution + direction
        resid = resid - apply_operator(direction)
        rho_next = 1.0 / (4.0 - rho)
        direction = (rho_next * rho) * direction + (4.0 * rho_next) * resid
        rho = rho_next
    return remerge(solution + direction)
```

```python
import functools

import jax
import jax.numpy as jnp
import numpy as np
from jax import lax
from jax.experimental import pallas as pl
from jax.experimental.pallas import tpu as pltpu
from jax.sharding import PartitionSpec as P

CHEB = 4
F32 = jnp.float32
BF16 = jnp.bfloat16


def split(value):
    high = value.astype(BF16)
    return high, (value - high.astype(F32)).astype(BF16)


def dot(left, right):
    return jnp.dot(left, right, preferred_element_type=F32)


def dot3(left_high, left_low, right):
    high, low = split(right)
    return dot(left_high, high) + dot(left_high, low) + dot(left_low, high)


def spanwise_tables(count):
    phase = np.arange(2 * count)[:, None] * np.arange(count)[None, :] % (2 * count)
    angle = 2.0 * np.pi / (2 * count) * phase
    weights = np.where(np.arange(count) == 0, 1.0, 2.0)[None, :, None]
    waves = np.stack([np.cos(angle), -np.sin(angle)], axis=2)
    forward = (weights * waves).reshape(2 * count, 2 * count).astype(np.float32)
    back = (waves / (2 * count)).reshape(2 * count, 2 * count).T.astype(np.float32)
    tables = []
    for table in (forward, back):
        high = table.astype(jnp.bfloat16)
        tables += [high, (table - high.astype(np.float32)).astype(jnp.bfloat16)]
    return tables


def lines_kernel(chunk, lines, inv_high, inv_low, back_high, back_low, diag, out):
    count = diag.shape[0]
    columns = lines.shape[-1]
    planes = []
    for field in range(2):
        for part in range(3):
            value = lines[:, field, part].reshape(count, columns)
            planes.append(dot3(inv_high[...], inv_low[...], value))
    for part in range(3):
        one, two = (part + 1) % 3, (part + 2) % 3
        cross = planes[one] * planes[3 + two] - planes[two] * planes[3 + one]
        forcing = dot3(back_high[...], back_low[...], cross)
        rhs = (lines[:, 0, part].reshape(count, columns) + forcing) * diag[...]
        if chunk % 8 == 0:
            out[:, part * chunk : (part + 1) * chunk, :] = rhs.reshape(count // chunk, chunk, columns)
        else:
            out[part] = rhs


def cheb_kernel(group, sides, refs, rhs, weights, scale, out, fields, resid, solution, rows_in, wide):
    sources, rows, columns = rhs.shape
    per_source = columns // 64
    elems = sources * per_source
    slots = rows_in.shape[1] // 64
    lane = lax.broadcasted_iota(jnp.int32, (1, 1, 128), 2)
    lower = lane < 64
    first, second = fields.at[0], fields.at[1]
    wide[:, :128], wide[:, 128:] = split(weights[...])
    for half in range(columns // 128):
        both = rhs[:, :, half * 128 : (half + 1) * 128]
        turned = pltpu.roll(both, 64, axis=2)
        first[:, 2 * half] = jnp.where(lower, both, turned)
        first[:, 2 * half + 1] = jnp.where(lower, turned, both)

    rho = 0.5
    for step in range(CHEB):
        now, later = (first, second) if step % 2 == 0 else (second, first)
        rho_next = 1.0 / (4.0 - rho)
        last = step == CHEB - 1

        def body(index, carry, step=step, now=now, later=later, rho=rho, rho_next=rho_next, last=last):
            low_lane = lower[0]
            for j in range(group):
                elem = index * group + j
                for pair in range(slots // 2):
                    a = refs[2 * pair, elem]
                    b = refs[2 * pair + 1, elem]
                    left = now[a // per_source, a % per_source]
                    right = now[b // per_source, b % per_source]
                    rows_in[j * rows : (j + 1) * rows, pair * 128 : (pair + 1) * 128] = jnp.where(
                        low_lane, left, right
                    )
            high, low = split(rows_in[...])
            total = dot(high, wide[...])
            total = total[:, :128] + total[:, 128:] + dot(low, wide[:, :128])
            total = total.reshape(group // per_source, per_source, rows, 128)
            here = pl.ds(index * (group // per_source), group // per_source)
            direction = now[here]
            old = direction if step == 0 else resid[here]
            new = old - (direction + scale[...] * total)
            ahead = rho_next * rho * direction + 4.0 * rho_next * new
            so_far = direction if step == 0 else solution[here] + direction
            if last:
                solution[here] = so_far + ahead
            else:
                resid[here] = new
                solution[here] = so_far
                later[here] = ahead
            return carry

        lax.fori_loop(0, elems // group, body, 0)
        rho = rho_next

    for behind in range(sources // sides):
        for half in range(columns // 128):
            at = behind * columns + half * 128
            here = pl.ds(behind * sides, sides)
            out[:, :, at : at + 128] = jnp.where(
                lower, solution[here, 2 * half], solution[here, 2 * half + 1]
            )


def shards(velocity, vorticity, blocks, nbr_ref, send_list):
    slot_count, points, _ = blocks.shape
    modes_dev, merged = velocity.shape[1], velocity.shape[3]
    mode_size, dom_size = lax.axis_size("mode"), lax.axis_size("dom")
    devices = mode_size * dom_size
    modes_all = modes_dev * mode_size
    count = 2 * modes_all
    columns = merged // mode_size
    elem_local = merged // points
    per_source = columns // points
    chunk = count // devices
    rows = 3 * chunk
    rows_up = -(-rows // 8) * 8

    tables = jnp.concatenate([nbr_ref.reshape(-1), send_list.reshape(-1)])
    tables = lax.all_gather(tables, "dom")
    refs = tables[:, : slot_count * elem_local].reshape(dom_size, slot_count, elem_local)
    lists = tables[:, slot_count * elem_local :].reshape(dom_size, 2, -1)
    doms = jnp.arange(dom_size, dtype=jnp.int32)[:, None]
    own = jnp.broadcast_to(jnp.arange(elem_local, dtype=jnp.int32)[None], (dom_size, elem_local))

    def place(dom, elem):
        return ((elem // per_source) * dom_size + dom) * per_source + elem % per_source

    extended = jnp.concatenate(
        [
            place(doms, own),
            jnp.roll(place(doms, lists[:, 0]), 1, axis=0),
            jnp.roll(place(doms, lists[:, 1]), -1, axis=0),
        ],
        axis=1,
    )
    entries = jnp.arange(extended.shape[1], dtype=jnp.int32)
    chosen = jnp.sum(
        jnp.where(refs[..., None] == entries, extended[:, None, None, :], 0), axis=-1
    )
    chosen = jnp.pad(chosen, ((0, 0), (0, slot_count % 2), (0, 0)))
    slots = chosen.shape[1]
    chosen = chosen.reshape(dom_size, slots, mode_size, per_source).transpose(1, 2, 0, 3)
    chosen = chosen.reshape(slots, devices * per_source)

    weights = jnp.swapaxes(blocks, 1, 2).reshape(slot_count * points, points)
    weights = jnp.pad(weights, ((0, (slots - slot_count) * points), (0, 0)))
    weights = jnp.concatenate([weights] * 2, axis=1)

    wavenum = np.arange(modes_all, dtype=np.float32) / np.float32(modes_all)
    inv_diag = np.repeat(np.float32(1.0) / (np.float32(1.0) + np.float32(4.0) * wavenum * wavenum), 2)

    both = jnp.stack([velocity, vorticity]).reshape(6 * modes_dev * 2, mode_size, columns)
    both = jnp.swapaxes(both, 0, 1)
    both = lax.all_to_all(both, "mode", split_axis=0, concat_axis=0, tiled=True)
    lines = both.reshape(mode_size, 2, 3, 2 * modes_dev, columns)

    aligned = chunk % 8 == 0
    rhs = pl.pallas_call(
        functools.partial(lines_kernel, chunk),
        out_shape=jax.ShapeDtypeStruct(
            (devices, rows, columns) if aligned else (3, count, columns), F32
        ),
        compiler_params=pltpu.CompilerParams(vmem_limit_bytes=40 * 2**20),
    )(lines, *(jnp.asarray(t) for t in spanwise_tables(modes_all)), jnp.asarray(inv_diag[:, None]))
    if not aligned:
        rhs = jnp.swapaxes(rhs.reshape(3, devices, chunk, columns), 0, 1).reshape(devices, rows, columns)
    rhs = lax.all_to_all(rhs, ("mode", "dom"), split_axis=0, concat_axis=0, tiled=True)
    if rows_up != rows:
        rhs = jnp.pad(rhs, ((0, 0), (0, rows_up - rows), (0, 0)))

    me = lax.axis_index("mode") * dom_size + lax.axis_index("dom")
    mode_ids = (me * chunk + jnp.arange(chunk, dtype=jnp.int32)) // 2
    wave = mode_ids.astype(F32) / modes_all
    scale = jnp.tile(1.0 / (1.0 + 4.0 * wave * wave), 3)
    scale = jnp.pad(scale, (0, rows_up - rows))
    scale = jnp.broadcast_to(scale[:, None], (rows_up, 128))

    group = 2 * per_source
    held = (devices, per_source, rows_up, 128)
    vmem = pl.BlockSpec(memory_space=pltpu.VMEM)
    out = pl.pallas_call(
        functools.partial(cheb_kernel, group, dom_size),
        out_shape=jax.ShapeDtypeStruct((dom_size, rows_up, merged), F32),
        in_specs=[pl.BlockSpec(memory_space=pltpu.SMEM)] + [vmem] * 3,
        out_specs=vmem,
        scratch_shapes=[
            pltpu.VMEM((2, *held), F32),
            pltpu.VMEM(held, F32),
            pltpu.VMEM(held, F32),
            pltpu.VMEM((group * rows_up, slots * points), F32),
            pltpu.VMEM((slots * points, 256), BF16),
        ],
        compiler_params=pltpu.CompilerParams(vmem_limit_bytes=48 * 2**20),
    )(chosen, rhs, weights, scale)
    out = lax.all_to_all(out[:, :rows], "dom", split_axis=0, concat_axis=0, tiled=True)
    out = jnp.swapaxes(out.reshape(dom_size, 3, chunk, merged), 0, 1)
    return out.reshape(3, modes_dev, 2, merged)


def solution(mesh):
    placed = (
        P(None, "mode", None, "dom"),
        P(None, "mode", None, "dom"),
        P(),
        P(None, "dom"),
        P(None, "dom"),
    )
    return jax.shard_map(
        shards, mesh=mesh, in_specs=placed, out_specs=P(None, "mode", None, "dom"), check_vma=False
    )
```

```python
import functools

import jax
import jax.numpy as jnp
import numpy as np
from jax import lax
from jax.experimental import pallas as pl
from jax.experimental.pallas import tpu as pltpu
from jax.sharding import PartitionSpec as P

CHEB = 4
F32 = jnp.float32
BF16 = jnp.bfloat16


def split(value):
    high = value.astype(BF16)
    return high, (value - high.astype(F32)).astype(BF16)


def dot(left, right):
    return jnp.dot(left, right, preferred_element_type=F32)


def dot3(left_high, left_low, right):
    high, low = split(right)
    return dot(left_high, high) + dot(left_high, low) + dot(left_low, high)


def spanwise_tables(count):
    phase = np.arange(2 * count)[:, None] * np.arange(count)[None, :] % (2 * count)
    angle = 2.0 * np.pi / (2 * count) * phase
    weights = np.where(np.arange(count) == 0, 1.0, 2.0)[None, :, None]
    waves = np.stack([np.cos(angle), -np.sin(angle)], axis=2)
    forward = (weights * waves).reshape(2 * count, 2 * count).astype(np.float32)
    back = (waves / (2 * count)).reshape(2 * count, 2 * count).T.astype(np.float32)
    tables = []
    for table in (forward, back):
        high = table.astype(jnp.bfloat16)
        tables += [high, (table - high.astype(np.float32)).astype(jnp.bfloat16)]
    return tables


def lines_kernel(chunk, lines, inv_high, inv_low, back_high, back_low, diag, out):
    count = diag.shape[0]
    columns = lines.shape[-1]
    planes = []
    for field in range(2):
        for part in range(3):
            value = lines[:, field, part].reshape(count, columns)
            planes.append(dot3(inv_high[...], inv_low[...], value))
    for part in range(3):
        one, two = (part + 1) % 3, (part + 2) % 3
        cross = planes[one] * planes[3 + two] - planes[two] * planes[3 + one]
        forcing = dot3(back_high[...], back_low[...], cross)
        rhs = (lines[:, 0, part].reshape(count, columns) + forcing) * diag[...]
        if chunk % 8 == 0:
            out[:, part * chunk : (part + 1) * chunk, :] = rhs.reshape(count // chunk, chunk, columns)
        else:
            out[part] = rhs


def cheb_kernel(group, sides, refs, rhs, weights, scale, out, fields, resid, solution, rows_in, wide):
    sources, rows, columns = rhs.shape
    per_source = columns // 64
    elems = sources * per_source
    slots = rows_in.shape[1] // 64
    lane = lax.broadcasted_iota(jnp.int32, (1, 1, 128), 2)
    lower = lane < 64
    first, second = fields.at[0], fields.at[1]
    wide[:, :128], wide[:, 128:] = split(weights[...])
    for half in range(columns // 128):
        both = rhs[:, :, half * 128 : (half + 1) * 128]
        turned = pltpu.roll(both, 64, axis=2)
        at = 2 * half * sources
        first[at : at + sources] = jnp.where(lower, both, turned)
        first[at + sources : at + 2 * sources] = jnp.where(lower, turned, both)

    rho = 0.5
    for step in range(CHEB):
        now, later = (first, second) if step % 2 == 0 else (second, first)
        rho_next = 1.0 / (4.0 - rho)
        last = step == CHEB - 1

        def body(index, carry, step=step, now=now, later=later, rho=rho, rho_next=rho_next, last=last):
            low_lane = lower[0]
            for j in range(group):
                elem = index * group + j
                for pair in range(slots // 2):
                    a = refs[2 * pair, elem]
                    b = refs[2 * pair + 1, elem]
                    left = now[a]
                    right = now[b]
                    rows_in[j * rows : (j + 1) * rows, pair * 128 : (pair + 1) * 128] = jnp.where(
                        low_lane, left, right
                    )
            high, low = split(rows_in[...])
            total = dot(high, wide[...])
            total = total[:, :128] + total[:, 128:] + dot(low, wide[:, :128])
            total = total.reshape(group, rows, 128)
            here = pl.ds(index * group, group)
            direction = now[here]
            old = direction if step == 0 else resid[here]
            new = old - (direction + scale[...] * total)
            ahead = rho_next * rho * direction + 4.0 * rho_next * new
            so_far = direction if step == 0 else solution[here] + direction
            if last:
                solution[here] = so_far + ahead
            else:
                resid[here] = new
                solution[here] = so_far
                later[here] = ahead
            return carry

        lax.fori_loop(0, elems // group, body, 0)
        rho = rho_next

    for behind in range(sources // sides):
        for half in range(columns // 128):
            at = behind * columns + half * 128
            even = pl.ds(2 * half * sources + behind * sides, sides)
            odd = pl.ds((2 * half + 1) * sources + behind * sides, sides)
            out[:, :, at : at + 128] = jnp.where(lower, solution[even], solution[odd])


def shards(velocity, vorticity, blocks, nbr_ref, send_list):
    slot_count, points, _ = blocks.shape
    modes_dev, merged = velocity.shape[1], velocity.shape[3]
    mode_size, dom_size = lax.axis_size("mode"), lax.axis_size("dom")
    devices = mode_size * dom_size
    modes_all = modes_dev * mode_size
    count = 2 * modes_all
    columns = merged // mode_size
    elem_local = merged // points
    per_source = columns // points
    chunk = count // devices
    rows = 3 * chunk
    rows_up = -(-rows // 8) * 8

    tables = jnp.concatenate([nbr_ref.reshape(-1), send_list.reshape(-1)])
    tables = lax.all_gather(tables, "dom")
    refs = tables[:, : slot_count * elem_local].reshape(dom_size, slot_count, elem_local)
    lists = tables[:, slot_count * elem_local :].reshape(dom_size, 2, -1)
    doms = jnp.arange(dom_size, dtype=jnp.int32)[:, None]
    own = jnp.broadcast_to(jnp.arange(elem_local, dtype=jnp.int32)[None], (dom_size, elem_local))

    def place(dom, elem):
        return (elem % per_source) * devices + (elem // per_source) * dom_size + dom

    extended = jnp.concatenate(
        [
            place(doms, own),
            jnp.roll(place(doms, lists[:, 0]), 1, axis=0),
            jnp.roll(place(doms, lists[:, 1]), -1, axis=0),
        ],
        axis=1,
    )
    entries = jnp.arange(extended.shape[1], dtype=jnp.int32)
    chosen = jnp.sum(
        jnp.where(refs[..., None] == entries, extended[:, None, None, :], 0), axis=-1
    )
    chosen = jnp.pad(chosen, ((0, 0), (0, slot_count % 2), (0, 0)))
    slots = chosen.shape[1]
    chosen = chosen.reshape(dom_size, slots, mode_size, per_source).transpose(1, 3, 2, 0)
    chosen = chosen.reshape(slots, devices * per_source)

    weights = jnp.swapaxes(blocks, 1, 2).reshape(slot_count * points, points)
    weights = jnp.pad(weights, ((0, (slots - slot_count) * points), (0, 0)))
    weights = jnp.concatenate([weights] * 2, axis=1)

    wavenum = np.arange(modes_all, dtype=np.float32) / np.float32(modes_all)
    inv_diag = np.repeat(np.float32(1.0) / (np.float32(1.0) + np.float32(4.0) * wavenum * wavenum), 2)

    both = jnp.stack([velocity, vorticity]).reshape(6 * modes_dev * 2, mode_size, columns)
    both = jnp.swapaxes(both, 0, 1)
    both = lax.all_to_all(both, "mode", split_axis=0, concat_axis=0, tiled=True)
    lines = both.reshape(mode_size, 2, 3, 2 * modes_dev, columns)

    aligned = chunk % 8 == 0
    rhs = pl.pallas_call(
        functools.partial(lines_kernel, chunk),
        out_shape=jax.ShapeDtypeStruct(
            (devices, rows, columns) if aligned else (3, count, columns), F32
        ),
        compiler_params=pltpu.CompilerParams(vmem_limit_bytes=40 * 2**20),
    )(lines, *(jnp.asarray(t) for t in spanwise_tables(modes_all)), jnp.asarray(inv_diag[:, None]))
    if not aligned:
        rhs = jnp.swapaxes(rhs.reshape(3, devices, chunk, columns), 0, 1).reshape(devices, rows, columns)
    rhs = lax.all_to_all(rhs, ("mode", "dom"), split_axis=0, concat_axis=0, tiled=True)
    if rows_up != rows:
        rhs = jnp.pad(rhs, ((0, 0), (0, rows_up - rows), (0, 0)))

    me = lax.axis_index("mode") * dom_size + lax.axis_index("dom")
    mode_ids = (me * chunk + jnp.arange(chunk, dtype=jnp.int32)) // 2
    wave = mode_ids.astype(F32) / modes_all
    scale = jnp.tile(1.0 / (1.0 + 4.0 * wave * wave), 3)
    scale = jnp.pad(scale, (0, rows_up - rows))
    scale = jnp.broadcast_to(scale[:, None], (rows_up, 128))

    group = min(32, devices)
    held = (devices * per_source, rows_up, 128)
    vmem = pl.BlockSpec(memory_space=pltpu.VMEM)
    out = pl.pallas_call(
        functools.partial(cheb_kernel, group, dom_size),
        out_shape=jax.ShapeDtypeStruct((dom_size, rows_up, merged), F32),
        in_specs=[pl.BlockSpec(memory_space=pltpu.SMEM)] + [vmem] * 3,
        out_specs=vmem,
        scratch_shapes=[
            pltpu.VMEM((2, *held), F32),
            pltpu.VMEM(held, F32),
            pltpu.VMEM(held, F32),
            pltpu.VMEM((group * rows_up, slots * points), F32),
            pltpu.VMEM((slots * points, 256), BF16),
        ],
        compiler_params=pltpu.CompilerParams(vmem_limit_bytes=48 * 2**20),
    )(chosen, rhs, weights, scale)
    out = lax.all_to_all(out[:, :rows], "dom", split_axis=0, concat_axis=0, tiled=True)
    out = jnp.swapaxes(out.reshape(dom_size, 3, chunk, merged), 0, 1)
    return out.reshape(3, modes_dev, 2, merged)


def solution(mesh):
    placed = (
        P(None, "mode", None, "dom"),
        P(None, "mode", None, "dom"),
        P(),
        P(None, "dom"),
        P(None, "dom"),
    )
    return jax.shard_map(
        shards, mesh=mesh, in_specs=placed, out_specs=P(None, "mode", None, "dom"), check_vma=False
    )
```

```python
import functools

import jax
import jax.numpy as jnp
import numpy as np
from jax import lax
from jax.experimental import pallas as pl
from jax.experimental.pallas import tpu as pltpu
from jax.sharding import PartitionSpec as P

CHEB = 4
PARTS = ((0, 2), (2, 3))
F32 = jnp.float32
BF16 = jnp.bfloat16


def split(value):
    high = value.astype(BF16)
    return high, (value - high.astype(F32)).astype(BF16)


def dot(left, right):
    return jnp.dot(left, right, preferred_element_type=F32)


def dot3(left_high, left_low, right):
    high, low = split(right)
    return dot(left_high, high) + dot(left_high, low) + dot(left_low, high)


def spanwise_tables(count):
    phase = np.arange(2 * count)[:, None] * np.arange(count)[None, :] % (2 * count)
    angle = 2.0 * np.pi / (2 * count) * phase
    weights = np.where(np.arange(count) == 0, 1.0, 2.0)[None, :, None]
    waves = np.stack([np.cos(angle), -np.sin(angle)], axis=2)
    forward = (weights * waves).reshape(2 * count, 2 * count).astype(np.float32)
    back = (waves / (2 * count)).reshape(2 * count, 2 * count).T.astype(np.float32)
    tables = []
    for table in (forward, back):
        high = table.astype(jnp.bfloat16)
        tables += [high, (table - high.astype(np.float32)).astype(jnp.bfloat16)]
    return tables


def lines_kernel(chunk, lines, inv_high, inv_low, back_high, back_low, diag, *outs):
    count = diag.shape[0]
    columns = lines.shape[-1]
    planes = []
    for field in range(2):
        for part in range(3):
            value = lines[:, field, part].reshape(count, columns)
            planes.append(dot3(inv_high[...], inv_low[...], value))
    for part in range(3):
        one, two = (part + 1) % 3, (part + 2) % 3
        cross = planes[one] * planes[3 + two] - planes[two] * planes[3 + one]
        forcing = dot3(back_high[...], back_low[...], cross)
        rhs = (lines[:, 0, part].reshape(count, columns) + forcing) * diag[...]
        for out, (begin, end) in zip(outs, PARTS):
            if begin <= part < end:
                at = part - begin
                if chunk % 8 == 0:
                    out[:, at * chunk : (at + 1) * chunk, :] = rhs.reshape(count // chunk, chunk, columns)
                else:
                    out[at] = rhs


def cheb_kernel(group, sides, refs, rhs, weights, scale, out, fields, resid, solution, rows_in, wide):
    sources, rows, columns = rhs.shape
    per_source = columns // 64
    elems = sources * per_source
    slots = rows_in.shape[1] // 64
    lane = lax.broadcasted_iota(jnp.int32, (1, 1, 128), 2)
    lower = lane < 64
    first, second = fields.at[0], fields.at[1]
    wide[:, :128], wide[:, 128:] = split(weights[...])
    for half in range(columns // 128):
        both = rhs[:, :, half * 128 : (half + 1) * 128]
        turned = pltpu.roll(both, 64, axis=2)
        at = 2 * half * sources
        first[at : at + sources] = jnp.where(lower, both, turned)
        first[at + sources : at + 2 * sources] = jnp.where(lower, turned, both)

    rho = 0.5
    for step in range(CHEB):
        now, later = (first, second) if step % 2 == 0 else (second, first)
        rho_next = 1.0 / (4.0 - rho)
        last = step == CHEB - 1

        def body(index, carry, step=step, now=now, later=later, rho=rho, rho_next=rho_next, last=last):
            low_lane = lower[0]
            for j in range(group):
                elem = index * group + j
                for pair in range(slots // 2):
                    a = refs[2 * pair, elem]
                    b = refs[2 * pair + 1, elem]
                    left = now[a]
                    right = now[b]
                    rows_in[j * rows : (j + 1) * rows, pair * 128 : (pair + 1) * 128] = jnp.where(
                        low_lane, left, right
                    )
            high, low = split(rows_in[...])
            total = dot(high, wide[...])
            total = total[:, :128] + total[:, 128:] + dot(low, wide[:, :128])
            total = total.reshape(group, rows, 128)
            here = pl.ds(index * group, group)
            direction = now[here]
            old = direction if step == 0 else resid[here]
            new = old - (direction + scale[...] * total)
            ahead = rho_next * rho * direction + 4.0 * rho_next * new
            so_far = direction if step == 0 else solution[here] + direction
            if last:
                solution[here] = so_far + ahead
            else:
                resid[here] = new
                solution[here] = so_far
                later[here] = ahead
            return carry

        lax.fori_loop(0, elems // group, body, 0)
        rho = rho_next

    for behind in range(sources // sides):
        for half in range(columns // 128):
            at = behind * columns + half * 128
            even = pl.ds(2 * half * sources + behind * sides, sides)
            odd = pl.ds((2 * half + 1) * sources + behind * sides, sides)
            out[:, :, at : at + 128] = jnp.where(lower, solution[even], solution[odd])


def shards(velocity, vorticity, blocks, nbr_ref, send_list):
    slot_count, points, _ = blocks.shape
    modes_dev, merged = velocity.shape[1], velocity.shape[3]
    mode_size, dom_size = lax.axis_size("mode"), lax.axis_size("dom")
    devices = mode_size * dom_size
    modes_all = modes_dev * mode_size
    count = 2 * modes_all
    columns = merged // mode_size
    elem_local = merged // points
    per_source = columns // points
    chunk = count // devices
    aligned = chunk % 8 == 0

    tables = jnp.concatenate([nbr_ref.reshape(-1), send_list.reshape(-1)])
    tables = lax.all_gather(tables, "dom")
    refs = tables[:, : slot_count * elem_local].reshape(dom_size, slot_count, elem_local)
    lists = tables[:, slot_count * elem_local :].reshape(dom_size, 2, -1)
    doms = jnp.arange(dom_size, dtype=jnp.int32)[:, None]
    own = jnp.broadcast_to(jnp.arange(elem_local, dtype=jnp.int32)[None], (dom_size, elem_local))

    def place(dom, elem):
        return (elem % per_source) * devices + (elem // per_source) * dom_size + dom

    extended = jnp.concatenate(
        [
            place(doms, own),
            jnp.roll(place(doms, lists[:, 0]), 1, axis=0),
            jnp.roll(place(doms, lists[:, 1]), -1, axis=0),
        ],
        axis=1,
    )
    entries = jnp.arange(extended.shape[1], dtype=jnp.int32)
    chosen = jnp.sum(
        jnp.where(refs[..., None] == entries, extended[:, None, None, :], 0), axis=-1
    )
    chosen = jnp.pad(chosen, ((0, 0), (0, slot_count % 2), (0, 0)))
    slots = chosen.shape[1]
    chosen = chosen.reshape(dom_size, slots, mode_size, per_source).transpose(1, 3, 2, 0)
    chosen = chosen.reshape(slots, devices * per_source)

    weights = jnp.swapaxes(blocks, 1, 2).reshape(slot_count * points, points)
    weights = jnp.pad(weights, ((0, (slots - slot_count) * points), (0, 0)))
    weights = jnp.concatenate([weights] * 2, axis=1)

    wavenum = np.arange(modes_all, dtype=np.float32) / np.float32(modes_all)
    inv_diag = np.repeat(np.float32(1.0) / (np.float32(1.0) + np.float32(4.0) * wavenum * wavenum), 2)

    both = jnp.stack([velocity, vorticity]).reshape(6 * modes_dev * 2, mode_size, columns)
    both = jnp.swapaxes(both, 0, 1)
    both = lax.all_to_all(both, "mode", split_axis=0, concat_axis=0, tiled=True)
    lines = both.reshape(mode_size, 2, 3, 2 * modes_dev, columns)

    made = pl.pallas_call(
        functools.partial(lines_kernel, chunk),
        out_shape=[
            jax.ShapeDtypeStruct(
                (devices, (end - begin) * chunk, columns) if aligned else (end - begin, count, columns), F32
            )
            for begin, end in PARTS
        ],
        compiler_params=pltpu.CompilerParams(vmem_limit_bytes=24 * 2**20),
        cost_estimate=pl.CostEstimate(flops=2 * 27 * count * count * columns, bytes_accessed=2**21, transcendentals=0),
    )(lines, *(jnp.asarray(t) for t in spanwise_tables(modes_all)), jnp.asarray(inv_diag[:, None]))

    me = lax.axis_index("mode") * dom_size + lax.axis_index("dom")
    mode_ids = (me * chunk + jnp.arange(chunk, dtype=jnp.int32)) // 2
    wave = mode_ids.astype(F32) / modes_all
    own_diag = 1.0 / (1.0 + 4.0 * wave * wave)
    vmem = pl.BlockSpec(memory_space=pltpu.VMEM)
    pieces = []
    made = list(made)
    for part, (begin, end) in enumerate(PARTS):
        rhs = made[part]
        rows = (end - begin) * chunk
        rows_up = -(-rows // 8) * 8
        if not aligned:
            rhs = jnp.swapaxes(rhs.reshape(end - begin, devices, chunk, columns), 0, 1)
            rhs = rhs.reshape(devices, rows, columns)
        rhs = lax.all_to_all(rhs, ("mode", "dom"), split_axis=0, concat_axis=0, tiled=True)
        if part + 1 < len(PARTS):
            rhs, made[part + 1] = lax.optimization_barrier((rhs, made[part + 1]))
        if rows_up != rows:
            rhs = jnp.pad(rhs, ((0, 0), (0, rows_up - rows), (0, 0)))
        scale = jnp.pad(jnp.tile(own_diag, end - begin), (0, rows_up - rows))
        scale = jnp.broadcast_to(scale[:, None], (rows_up, 128))
        group = min(32, devices)
        held = (devices * per_source, rows_up, 128)
        out = pl.pallas_call(
            functools.partial(cheb_kernel, group, dom_size),
            out_shape=jax.ShapeDtypeStruct((dom_size, rows_up, merged), F32),
            in_specs=[pl.BlockSpec(memory_space=pltpu.SMEM)] + [vmem] * 3,
            out_specs=vmem,
            scratch_shapes=[
                pltpu.VMEM((2, *held), F32),
                pltpu.VMEM(held, F32),
                pltpu.VMEM(held, F32),
                pltpu.VMEM((group * rows_up, slots * points), F32),
                pltpu.VMEM((slots * points, 256), BF16),
            ],
            compiler_params=pltpu.CompilerParams(vmem_limit_bytes=32 * 2**20),
            cost_estimate=pl.CostEstimate(
                flops=rows_up * 4 * 10**8, bytes_accessed=2**20, transcendentals=0
            ),
        )(chosen, rhs, weights, scale)
        out = lax.all_to_all(out[:, :rows], "dom", split_axis=0, concat_axis=0, tiled=True)
        pieces.append(jnp.swapaxes(out.reshape(dom_size, end - begin, chunk, merged), 0, 1))
    return jnp.concatenate(pieces, axis=0).reshape(3, modes_dev, 2, merged)


def solution(mesh):
    placed = (
        P(None, "mode", None, "dom"),
        P(None, "mode", None, "dom"),
        P(),
        P(None, "dom"),
        P(None, "dom"),
    )
    return jax.shard_map(
        shards, mesh=mesh, in_specs=placed, out_specs=P(None, "mode", None, "dom"), check_vma=False
    )
```

```python
import functools

import jax
import jax.numpy as jnp
import numpy as np
from jax import lax
from jax.experimental import pallas as pl
from jax.experimental.pallas import tpu as pltpu
from jax.sharding import PartitionSpec as P

CHEB = 4
F32 = jnp.float32
BF16 = jnp.bfloat16


def split(value):
    high = value.astype(BF16)
    return high, (value - high.astype(F32)).astype(BF16)


def dot(left, right):
    return jnp.dot(left, right, preferred_element_type=F32)


def dot3(left_high, left_low, right):
    high, low = split(right)
    return dot(left_high, high) + dot(left_high, low) + dot(left_low, high)


def spanwise_tables(count):
    phase = np.arange(2 * count)[:, None] * np.arange(count)[None, :] % (2 * count)
    angle = 2.0 * np.pi / (2 * count) * phase
    weights = np.where(np.arange(count) == 0, 1.0, 2.0)[None, :, None]
    waves = np.stack([np.cos(angle), -np.sin(angle)], axis=2)
    forward = (weights * waves).reshape(2 * count, 2 * count).astype(np.float32)
    back = (waves / (2 * count)).reshape(2 * count, 2 * count).T.astype(np.float32)
    tables = []
    for table in (forward, back):
        high = table.astype(jnp.bfloat16)
        tables += [high, (table - high.astype(np.float32)).astype(jnp.bfloat16)]
    return tables


def lines_kernel(chunk, lines, inv_high, inv_low, back_high, back_low, diag, out):
    count = diag.shape[0]
    columns = lines.shape[-1]
    planes = []
    for field in range(2):
        for part in range(3):
            value = lines[:, field, part].reshape(count, columns)
            planes.append(dot3(inv_high[...], inv_low[...], value))
    for part in range(3):
        one, two = (part + 1) % 3, (part + 2) % 3
        cross = planes[one] * planes[3 + two] - planes[two] * planes[3 + one]
        forcing = dot3(back_high[...], back_low[...], cross)
        rhs = (lines[:, 0, part].reshape(count, columns) + forcing) * diag[...]
        if chunk % 8 == 0:
            out[:, part * chunk : (part + 1) * chunk, :] = rhs.reshape(count // chunk, chunk, columns)
        else:
            out[part] = rhs


def cheb_kernel(group, sides, refs, rhs, weights, scale, out, fields, resid, solution, rows_in, wide):
    sources, rows, columns = rhs.shape
    per_source = columns // 64
    elems = sources * per_source
    slots = rows_in.shape[1] // 64
    used = refs.shape[0] // elems
    lane = lax.broadcasted_iota(jnp.int32, (1, 1, 128), 2)
    lower = lane < 64
    first, second = fields.at[0], fields.at[1]
    wide[:, :128], wide[:, 128:] = split(weights[...])
    for half in range(columns // 128):
        both = rhs[:, :, half * 128 : (half + 1) * 128]
        turned = pltpu.roll(both, 64, axis=2)
        at = 2 * half * sources
        first[at : at + sources] = jnp.where(lower, both, turned)
        first[at + sources : at + 2 * sources] = jnp.where(lower, turned, both)

    rho = 0.5
    for step in range(CHEB):
        now, later = (first, second) if step % 2 == 0 else (second, first)
        rho_next = 1.0 / (4.0 - rho)
        last = step == CHEB - 1

        def body(index, carry, step=step, now=now, later=later, rho=rho, rho_next=rho_next, last=last):
            low_lane = lower[0]
            base = index * (group * used)
            for j in range(group):
                for pair in range(slots // 2):
                    at = base + (j * used + 2 * pair)
                    value = now[refs[at]]
                    if 2 * pair + 1 < used:
                        value = jnp.where(low_lane, value, now[refs[at + 1]])
                    rows_in[j * rows : (j + 1) * rows, pair * 128 : (pair + 1) * 128] = value
            high, low = split(rows_in[...])
            total = dot(high, wide[...])
            total = total[:, :128] + total[:, 128:] + dot(low, wide[:, :128])
            total = total.reshape(group, rows, 128)
            here = pl.ds(index * group, group)
            direction = now[here]
            old = direction if step == 0 else resid[here]
            new = old - (direction + scale[...] * total)
            ahead = rho_next * rho * direction + 4.0 * rho_next * new
            so_far = direction if step == 0 else solution[here] + direction
            if last:
                solution[here] = so_far + ahead
            else:
                resid[here] = new
                solution[here] = so_far
                later[here] = ahead
            return carry

        lax.fori_loop(0, elems // group, body, 0)
        rho = rho_next

    for behind in range(sources // sides):
        for half in range(columns // 128):
            at = behind * columns + half * 128
            even = pl.ds(2 * half * sources + behind * sides, sides)
            odd = pl.ds((2 * half + 1) * sources + behind * sides, sides)
            out[:, :, at : at + 128] = jnp.where(lower, solution[even], solution[odd])


def shards(velocity, vorticity, blocks, nbr_ref, send_list):
    slot_count, points, _ = blocks.shape
    modes_dev, merged = velocity.shape[1], velocity.shape[3]
    mode_size, dom_size = lax.axis_size("mode"), lax.axis_size("dom")
    devices = mode_size * dom_size
    modes_all = modes_dev * mode_size
    count = 2 * modes_all
    columns = merged // mode_size
    elem_local = merged // points
    per_source = columns // points
    chunk = count // devices
    rows = 3 * chunk
    rows_up = -(-rows // 8) * 8

    tables = jnp.concatenate([nbr_ref.reshape(-1), send_list.reshape(-1)])
    tables = lax.all_gather(tables, "dom")
    refs = tables[:, : slot_count * elem_local].reshape(dom_size, slot_count, elem_local)
    lists = tables[:, slot_count * elem_local :].reshape(dom_size, 2, -1)
    doms = jnp.arange(dom_size, dtype=jnp.int32)[:, None]
    own = jnp.broadcast_to(jnp.arange(elem_local, dtype=jnp.int32)[None], (dom_size, elem_local))

    def place(dom, elem):
        return (elem % per_source) * devices + (elem // per_source) * dom_size + dom

    extended = jnp.concatenate(
        [
            place(doms, own),
            jnp.roll(place(doms, lists[:, 0]), 1, axis=0),
            jnp.roll(place(doms, lists[:, 1]), -1, axis=0),
        ],
        axis=1,
    )
    entries = jnp.arange(extended.shape[1], dtype=jnp.int32)
    chosen = jnp.sum(
        jnp.where(refs[..., None] == entries, extended[:, None, None, :], 0), axis=-1
    )
    slots = slot_count + slot_count % 2
    chosen = chosen.reshape(dom_size, slot_count, mode_size, per_source).transpose(3, 2, 0, 1)
    chosen = chosen.reshape(-1)

    weights = jnp.swapaxes(blocks, 1, 2).reshape(slot_count * points, points)
    weights = jnp.pad(weights, ((0, (slots - slot_count) * points), (0, 0)))
    weights = jnp.concatenate([weights] * 2, axis=1)

    wavenum = np.arange(modes_all, dtype=np.float32) / np.float32(modes_all)
    inv_diag = np.repeat(np.float32(1.0) / (np.float32(1.0) + np.float32(4.0) * wavenum * wavenum), 2)

    both = jnp.stack([velocity, vorticity]).reshape(6 * modes_dev * 2, mode_size, columns)
    both = jnp.swapaxes(both, 0, 1)
    both = lax.all_to_all(both, "mode", split_axis=0, concat_axis=0, tiled=True)
    lines = both.reshape(mode_size, 2, 3, 2 * modes_dev, columns)

    aligned = chunk % 8 == 0
    rhs = pl.pallas_call(
        functools.partial(lines_kernel, chunk),
        out_shape=jax.ShapeDtypeStruct(
            (devices, rows, columns) if aligned else (3, count, columns), F32
        ),
        compiler_params=pltpu.CompilerParams(vmem_limit_bytes=40 * 2**20),
    )(lines, *(jnp.asarray(t) for t in spanwise_tables(modes_all)), jnp.asarray(inv_diag[:, None]))
    if not aligned:
        rhs = jnp.swapaxes(rhs.reshape(3, devices, chunk, columns), 0, 1).reshape(devices, rows, columns)
    rhs = lax.all_to_all(rhs, ("mode", "dom"), split_axis=0, concat_axis=0, tiled=True)
    if rows_up != rows:
        rhs = jnp.pad(rhs, ((0, 0), (0, rows_up - rows), (0, 0)))

    me = lax.axis_index("mode") * dom_size + lax.axis_index("dom")
    mode_ids = (me * chunk + jnp.arange(chunk, dtype=jnp.int32)) // 2
    wave = mode_ids.astype(F32) / modes_all
    scale = jnp.tile(1.0 / (1.0 + 4.0 * wave * wave), 3)
    scale = jnp.pad(scale, (0, rows_up - rows))
    scale = jnp.broadcast_to(scale[:, None], (rows_up, 128))

    group = min(64, 2 * devices)
    held = (devices * per_source, rows_up, 128)
    vmem = pl.BlockSpec(memory_space=pltpu.VMEM)
    out = pl.pallas_call(
        functools.partial(cheb_kernel, group, dom_size),
        out_shape=jax.ShapeDtypeStruct((dom_size, rows_up, merged), F32),
        in_specs=[pl.BlockSpec(memory_space=pltpu.SMEM)] + [vmem] * 3,
        out_specs=vmem,
        scratch_shapes=[
            pltpu.VMEM((2, *held), F32),
            pltpu.VMEM(held, F32),
            pltpu.VMEM(held, F32),
            pltpu.VMEM((group * rows_up, slots * points), F32),
            pltpu.VMEM((slots * points, 256), BF16),
        ],
        compiler_params=pltpu.CompilerParams(vmem_limit_bytes=48 * 2**20),
    )(chosen, rhs, weights, scale)
    out = lax.all_to_all(out[:, :rows], "dom", split_axis=0, concat_axis=0, tiled=True)
    out = jnp.swapaxes(out.reshape(dom_size, 3, chunk, merged), 0, 1)
    return out.reshape(3, modes_dev, 2, merged)


def solution(mesh):
    placed = (
        P(None, "mode", None, "dom"),
        P(None, "mode", None, "dom"),
        P(),
        P(None, "dom"),
        P(None, "dom"),
    )
    return jax.shard_map(
        shards, mesh=mesh, in_specs=placed, out_specs=P(None, "mode", None, "dom"), check_vma=False
    )
```
